512 devices in a mesh: shot: 16 (over z_hi, y, core), rcv: 32 (over z_lo, x).
Axes of the slice: x: 4, y: 4, z: 16 (z_hi: 2, z_lo: 8; z = z_hi * 8 + z_lo), core: 2. Of those that a mesh axis runs over, the one named last changes fastest.
Arguments:
- traces: bfloat16 [1024, 1024, 512], P('shot', 'rcv'), may hold values from -6 to 6
- taper_weights: float32 [512], replicated, may hold values from 0.2 to 1
Outputs:
- multiples: bfloat16 [1024, 1024, 512], P('shot', 'rcv')
The draws below stay inside these ranges and needn't reach their ends.
All inputs are finite; a program needn't handle non-finite values.
Results may differ from the reference program's by a relative error of at most 0.0057.
Values may be sent and summed in bfloat16 or wider, within the bound.
A program may use at most 64 MiB of HBM per device.

```python
import math
import jax
import jax.numpy as jnp
from jax import lax

SHOT_DEV = 64
T_SIZE = 512
FREQ = 8
NSHOT = 1024


def block_scale(own_key, extent, cuts, smallest, high):
    gain, own = 1.0, jax.random.fold_in(own_key, 6)
    for axis_at, parts in cuts:
        steps = jnp.exp(jax.random.uniform(jax.random.fold_in(own, axis_at), (parts,), jnp.float32, smallest / len(cuts), high / len(cuts)))
        gain = gain * jnp.repeat(steps, extent[axis_at] // parts).reshape([-1 if axis == axis_at else 1 for axis in range(len(extent))])
    return gain


def gaussian(own_key, extent, scale, bound, shards=(), kind=jnp.bfloat16):
    level = block_scale(own_key, extent, shards, -0.22, 0.18) if shards else 1.0
    drawn = jax.random.normal(own_key, extent, jnp.float32) * scale * level
    return jnp.minimum(jnp.maximum(drawn, -bound), bound).astype(kind)


def setup_inputs(seed: int = 0) -> dict:
    key_list = jax.random.split(jax.random.key(seed), 3)
    traces = gaussian(key_list[0], (NSHOT, NSHOT, T_SIZE), 1.0, 6.0, ((0, 16), (1, 32)))
    taper_weights = jnp.clip(jax.random.uniform(key_list[1], (T_SIZE,), jnp.float32, 0.2, 1.0), 0.2, 1.0)
    return dict(traces=traces, taper_weights=taper_weights)


def fourier_kernel():
    samples = jnp.arange(T_SIZE, dtype=jnp.int32)
    freq_bins = 1 + 3 * jnp.arange(FREQ, dtype=jnp.int32)
    phases = 2.0 * math.pi * (freq_bins[:, None] * samples[None, :] % T_SIZE).astype(jnp.float32) / T_SIZE
    return jnp.stack([jnp.cos(phases), -jnp.sin(phases)])

def reference(traces, taper_weights):
    basis = fourier_kernel()
    weights = taper_weights[None, None, :] * basis / math.sqrt(T_SIZE)
    blocks = NSHOT // SHOT_DEV
    shaped = traces.reshape(blocks, SHOT_DEV, NSHOT, T_SIZE)

    def transform(block):
        return jnp.einsum('srt,cft->cfsr', block.astype(jnp.float32), weights, precision=lax.Precision.HIGHEST).astype(jnp.bfloat16)
    pieces_spec = lax.map(transform, shaped)
    spectra = jnp.concatenate([pieces_spec[index] for index in range(blocks)], axis=2)
    complete_real = spectra[0].astype(jnp.float32)
    complete_imaginary = spectra[1].astype(jnp.float32)

    def one_block(index):
        offset = (index * SHOT_DEV).astype(jnp.int32)
        row_real_values = lax.dynamic_slice_in_dim(complete_real, offset, SHOT_DEV, 1)
        row_imaginary = lax.dynamic_slice_in_dim(complete_imaginary, offset, SHOT_DEV, 1)
        product_real_values = jnp.einsum('uva,uae->uve', row_real_values, complete_real) - jnp.einsum('uva,uae->uve', row_imaginary, complete_imaginary)
        product_imaginary = jnp.einsum('uva,uae->uve', row_real_values, complete_imaginary) + jnp.einsum('uva,uae->uve', row_imaginary, complete_real)
        product = jnp.stack([product_real_values, product_imaginary]) / math.sqrt(NSHOT)
        timed = jnp.einsum('cfsr,cft->srt', product, basis, precision=lax.Precision.HIGHEST) / math.sqrt(FREQ)
        return timed.astype(jnp.bfloat16)
    pieces = lax.map(one_block, jnp.arange(blocks, dtype=jnp.int32))
    return pieces.reshape(NSHOT, NSHOT, T_SIZE)
```

```python
import functools
import math

import jax
import jax.numpy as jnp
import numpy as np
from jax import lax
from jax.experimental import pallas as pl
from jax.experimental.pallas import tpu as pltpu
from jax.sharding import PartitionSpec as P

FREQ = 8
MESH = pl.DeviceIdType.MESH
BF16, F32 = jnp.bfloat16, jnp.float32


def fourier_table(samples_count):
    samples = np.arange(samples_count)
    freq_bins = 1 + 3 * np.arange(FREQ)
    phases = 2.0 * math.pi * (freq_bins[:, None] * samples[None, :] % samples_count) / samples_count
    return np.concatenate([np.cos(phases), -np.sin(phases)]).astype(np.float32)


def place():
    shot, rcv = lax.axis_index("shot"), lax.axis_index("rcv")
    return lax.rem(rcv, 4), lax.rem(shot // 2, 4), shot // 8 * 8 + rcv // 4, lax.rem(shot, 2)


def device(x, y, z, core):
    return (z // 8 * 8 + y * 2 + core, lax.rem(z, 8) * 4 + x)


def ring(value, size):
    return lax.rem(value + size, size)


def split_in_two(value):
    high = value.astype(BF16)
    return high, (value - high.astype(F32)).astype(BF16)


def swap_quarters(tiles):
    quarter = lax.broadcasted_iota(jnp.int32, tiles[0].shape, 1) // 32
    out = []
    for j in range(4):
        total = None
        for i in range(4):
            shift = 32 * ((i - j) % 4)
            moved = pltpu.roll(tiles[i], shift, 1) if shift else tiles[i]
            total = moved if total is None else jnp.where(quarter == i, moved, total)
        out.append(total)
    return out


def product_kernel(
    traces, taper, basis, m_ref,
    tr, by_s, zsend, zin, own, a_buf, b_buf, c_out, c_in, c_own, zret,
    t_sem, zs_sem, zr_sem, as_sem, ar_sem, bs_sem, br_sem, cs_sem, cr_sem, rs_sem, rr_sem,
):
    x, y, z, core = place()
    pair = z // 2
    active = lax.rem(z, 2) == 0
    x_half, x_core = lax.rem(x, 2), x // 2
    samples = traces.shape[-1]

    def remote(src, dst, send, recv, target):
        return pltpu.make_async_remote_copy(
            src_ref=src, dst_ref=dst, send_sem=send, recv_sem=recv, device_id=target, device_id_type=MESH
        )

    barrier = pltpu.get_barrier_semaphore()

    def greet(target):
        pl.semaphore_signal(barrier, inc=1, device_id=target, device_id_type=MESH)

    @pl.when(active)
    def _():
        for step in (8, 7, 9, 6, 10, 5, 11, 4, 12, 3, 13, 2, 14, 1, 15):
            greet(device(x, y, lax.rem(z + step, 16), core))
        for step in (2, 1, 3):
            for other in (0, 1):
                greet(device(lax.rem(x + step, 4), y, z, other))
            greet(device(x, lax.rem(y + step, 4), z, core))
        greet(device(x, y, z, 1 - core))

    @pl.when(jnp.logical_not(active))
    def _():
        for step in (4, 3, 5, 2, 6, 1, 7, 0):
            greet(device(x, y, 2 * lax.rem(pair + step, 8), core))

    chunks = t_sem.shape[0]
    per_chunk = 16 // chunks

    def load(chunk):
        rows = pl.ds(chunk * per_chunk, per_chunk)
        return pltpu.make_async_copy(traces.at[:, rows], tr.at[:, rows], t_sem.at[chunk])

    for chunk in range(chunks):
        load(chunk).start()
    high, low = split_in_two(basis[...] * taper[...] / math.sqrt(samples))
    weights = jnp.concatenate([high, low])
    for s in range(0, 16, 2):
        if s % per_chunk == 0:
            load(s // per_chunk).wait()
        block = jnp.concatenate([tr[:, s], tr[:, s + 1]]).reshape(256, samples)
        both = lax.dot_general(weights, block, (((1,), (1,)), ((), ())), preferred_element_type=F32)
        summed = both[:16] + both[16:]
        by_s[pl.ds(s * 16, 16)] = summed[:, :128]
        by_s[pl.ds(s * 16 + 16, 16)] = summed[:, 128:]
    for freq in range(FREQ):
        for part in range(2):
            zsend[freq, part] = by_s[pl.ds(part * FREQ + freq, 16, stride=16), :].astype(BF16)

    @pl.when(active)
    def _():
        pl.semaphore_wait(barrier, 15 + 9 + 1)

    @pl.when(jnp.logical_not(active))
    def _():
        pl.semaphore_wait(barrier, 8)

    far_first = (4, 3, 5, 2, 6, 1, 7, 0)

    def to_plane(step):
        freq = lax.rem(pair + step, 8)
        return remote(
            zsend.at[freq], zin.at[z], zs_sem.at[step], zr_sem.at[z], device(x, y, 2 * freq, core)
        )

    for step in far_first[:-1]:
        to_plane(step).start()

    @pl.when(jnp.logical_not(active))
    def _():
        to_plane(0).start()

    def product_of_plane():
        zin[z] = zsend[pair]

        def a_copy(group, step):
            return remote(
                own.at[group], a_buf.at[x_half, group, core], as_sem.at[group, step], ar_sem.at[x_half, core, group],
                device(lax.rem(x + step, 4), y, z, x_core),
            )

        def b_copy(group, step):
            return remote(
                own.at[group], b_buf.at[group, :, :, y], bs_sem.at[group, step], br_sem.at[y, group],
                device(x, lax.rem(y + step, 4), z, core),
            )

        @pl.loop(0, 4)
        def _(index):
            group = lax.rem(z // 4 + (index ^ (index // 2)), 4)
            for i in range(4):
                source = group * 4 + i

                @pl.when(source != z)
                def _():
                    remote(
                        zsend.at[0], zin.at[source], zs_sem.at[0], zr_sem.at[source], device(x, y, z, core)
                    ).wait_recv()

            for part in range(2):
                tiles = swap_quarters([zin[group * 4 + i, part].astype(F32) for i in range(4)])
                for j in range(4):
                    tile = tiles[j].astype(BF16)
                    rows = pl.ds(j % 2 * 16, 16)
                    own[group, part, j // 2, rows] = tile
                    b_buf[group, part, j // 2, y, rows] = tile
            for step in (2, 1, 3):
                a_copy(group, step).start()
                b_copy(group, step).start()

            @pl.when(x_core != core)
            def _():
                a_copy(group, 0).start()

            @pl.when(x_core == core)
            def _():
                a_buf[x_half, group, core] = own[group]

        @pl.loop(0, 4)
        def _(group):
            for half in range(2):
                for other in range(2):

                    @pl.when(jnp.logical_or(x != 2 * core + half, other != core))
                    def _():
                        remote(
                            own.at[0], a_buf.at[half, group, other], as_sem.at[0, 0], ar_sem.at[half, other, group],
                            device(x, y, z, core),
                        ).wait_recv()

            for step in (1, 2, 3):
                row = lax.rem(y + step, 4)
                remote(
                    own.at[0], b_buf.at[group, :, :, row], bs_sem.at[0, 0], br_sem.at[row, group],
                    device(x, y, z, core),
                ).wait_recv()

        def right(part):
            return jnp.concatenate(
                [
                    jnp.concatenate(
                        [b_buf[2 * deep + wide, part, half].reshape(128, 128) for wide in range(2)], axis=1
                    )
                    for half in range(2)
                    for deep in range(2)
                ]
            )

        def left(rows_of, part, upper):
            return jnp.concatenate(
                [
                    a_buf[half, 2 * upper + deep, rows_of, part].reshape(64, 128)
                    for half in range(2)
                    for deep in range(2)
                ],
                axis=1,
            )

        def multiply(rows_of, out):
            rows = jnp.concatenate([left(rows_of, part, upper) for part in range(2) for upper in range(2)])
            by_real = jnp.dot(rows, right(0), preferred_element_type=F32)
            by_imag = jnp.dot(rows, right(1), preferred_element_type=F32)
            out[0] = by_real[:128] - by_imag[128:]
            out[1] = by_imag[:128] + by_real[128:]

        to_partner = remote(c_out, c_in, cs_sem, cr_sem, device(x, y, z, 1 - core))
        multiply(1 - core, c_out)
        to_partner.start()
        multiply(core, c_own)
        to_partner.wait_recv()

        def back(target, slot):
            return remote(
                zret.at[target], m_ref.at[pair], rs_sem.at[slot], rr_sem.at[pair], device(x, y, target, core)
            )

        @pl.loop(0, 4)
        def _(index):
            group = lax.rem(z // 4 + 2 + (index ^ (index // 2)), 4)
            upper, wide = group // 2, lax.rem(group, 2)
            lanes = pl.ds(pl.multiple_of(wide * 128, 128), 128)
            for part in range(2):
                tiles = []
                for j in range(4):
                    rows = pl.ds(pl.multiple_of(upper * 64 + j * 16, 16), 16)
                    tiles.append(c_own[part, rows, lanes] + c_in[part, rows, lanes])
                tiles = swap_quarters(tiles)
                for i in range(4):
                    zret[group * 4 + i, part] = (tiles[i] * (1.0 / 32.0)).astype(BF16)
            for i in range(4):
                target = group * 4 + i

                @pl.when(target != z)
                def _():
                    back(target, target).start()

        m_ref[pair] = zret[z]
        to_partner.wait_send()

        @pl.loop(0, 4)
        def _(group):
            for step in (1, 2, 3):
                a_copy(group, step).wait_send()
                b_copy(group, step).wait_send()

            @pl.when(x_core != core)
            def _():
                a_copy(group, 0).wait_send()

        @pl.loop(0, 16)
        def _(target):
            @pl.when(target != z)
            def _():
                back(target, target).wait_send()

    pl.when(active)(product_of_plane)

    for step in far_first[:-1]:
        to_plane(step).wait_send()

    @pl.when(jnp.logical_not(active))
    def _():
        to_plane(0).wait_send()

    for freq in range(FREQ):

        @pl.when(2 * freq != z)
        def _():
            remote(
                zret.at[0], m_ref.at[freq], rs_sem.at[0], rr_sem.at[freq], device(x, y, z, core)
            ).wait_recv()


def time_kernel(m_ref, basis, out, by_cf):
    @pl.when(pl.program_id(0) == 0)
    def _():
        for freq in range(FREQ):
            for part in range(2):
                by_cf[pl.ds((part * FREQ + freq) * 16, 16)] = m_ref[freq, part].astype(F32)

    high, low = split_in_two(basis[...] * (1.0 / math.sqrt(FREQ)))
    weights = jnp.concatenate([high, low])
    width = out.shape[1]
    for i in range(width):
        s = pl.program_id(0) * width + i
        rows = by_cf[pl.ds(s, 16, stride=16), :].astype(BF16)
        rows = jnp.concatenate([rows, rows])
        timed = lax.dot_general(rows, weights, (((0,), (0,)), ((), ())), preferred_element_type=F32)
        out[:, i] = timed.astype(BF16).reshape(4, 32, out.shape[-1])


def on_device(traces, taper_weights):
    shots, receivers, samples = traces.shape
    table = fourier_table(samples)
    vmem = pl.BlockSpec(memory_space=pltpu.VMEM)
    dma = pltpu.SemaphoreType.DMA
    product = pl.pallas_call(
        product_kernel,
        out_shape=jax.ShapeDtypeStruct((FREQ, 2, 16, 128), BF16),
        in_specs=[pl.BlockSpec(memory_space=pl.ANY), vmem, vmem],
        out_specs=vmem,
        scratch_shapes=[
            pltpu.VMEM((4, 16, receivers, samples), BF16),
            pltpu.VMEM((256, 128), F32),
            pltpu.VMEM((FREQ, 2, 16, 128), BF16),
            pltpu.VMEM((16, 2, 16, 128), BF16),
            pltpu.VMEM((4, 2, 2, 32, 128), BF16),
            pltpu.VMEM((2, 4, 2, 2, 2, 32, 128), BF16),
            pltpu.VMEM((4, 2, 2, 4, 32, 128), BF16),
            pltpu.VMEM((2, 128, 256), F32),
            pltpu.VMEM((2, 128, 256), F32),
            pltpu.VMEM((2, 128, 256), F32),
            pltpu.VMEM((16, 2, 16, 128), BF16),
            dma((4,)), dma((8,)), dma((16,)), dma((4, 4)), dma((2, 2, 4)), dma((4, 4)), dma((4, 4)),
            dma, dma, dma((16,)), dma((8,)),
        ],
        compiler_params=pltpu.CompilerParams(
            collective_id=0, has_side_effects=True, vmem_limit_bytes=32 << 20
        ),
        name="product",
    )(traces.reshape(4, 16, receivers, samples), taper_weights.reshape(1, samples), table)
    steps = 4
    timed = pl.pallas_call(
        time_kernel,
        grid=(steps,),
        out_shape=jax.ShapeDtypeStruct((4, 16, receivers, samples), BF16),
        in_specs=[
            pl.BlockSpec((FREQ, 2, 16, 128), lambda i: (0, 0, 0, 0)),
            pl.BlockSpec((2 * FREQ, samples), lambda i: (0, 0)),
        ],
        out_specs=pl.BlockSpec((4, 16 // steps, receivers, samples), lambda i: (0, i, 0, 0)),
        scratch_shapes=[pltpu.VMEM((256, 128), F32)],
        compiler_params=pltpu.CompilerParams(vmem_limit_bytes=32 << 20),
        name="back_to_time",
    )(product, table)
    return timed.reshape(shots, receivers, samples)


def solution(mesh):
    placed = (P("shot", "rcv", None), P())
    return jax.shard_map(
        on_device, mesh=mesh, in_specs=placed, out_specs=P("shot", "rcv", None), check_vma=False
    )
```

```python
import functools
import math

import jax
import jax.numpy as jnp
import numpy as np
from jax import lax
from jax.experimental import pallas as pl
from jax.experimental.pallas import tpu as pltpu
from jax.sharding import PartitionSpec as P

FREQ = 8
MESH = pl.DeviceIdType.MESH
BF16, F32 = jnp.bfloat16, jnp.float32


def fourier_table(samples_count):
    samples = np.arange(samples_count)
    freq_bins = 1 + 3 * np.arange(FREQ)
    phases = 2.0 * math.pi * (freq_bins[:, None] * samples[None, :] % samples_count) / samples_count
    return np.concatenate([np.cos(phases), -np.sin(phases)]).astype(np.float32)


def fourier_rows(samples_count):
    row = lax.broadcasted_iota(jnp.int32, (2 * FREQ, samples_count), 0)
    sample = lax.broadcasted_iota(jnp.int32, (2 * FREQ, samples_count), 1)
    quarters = 1 + row // FREQ
    turns = (1 + 3 * (row % FREQ)) * sample + quarters * (samples_count // 4) + samples_count // 2
    turns = turns % samples_count - samples_count // 2
    return jnp.sin(turns.astype(F32) * (2.0 * math.pi / samples_count))


def place():
    shot, rcv = lax.axis_index("shot"), lax.axis_index("rcv")
    return lax.rem(rcv, 4), lax.rem(shot // 2, 4), shot // 8 * 8 + rcv // 4, lax.rem(shot, 2)


def device(x, y, z, core):
    return (z // 8 * 8 + y * 2 + core, lax.rem(z, 8) * 4 + x)


def ring(value, size):
    return lax.rem(value + size, size)


def split_in_two(value):
    high = value.astype(BF16)
    return high, (value - high.astype(F32)).astype(BF16)


def swap_quarters(tiles):
    quarter = lax.broadcasted_iota(jnp.int32, tiles[0].shape, 1) // 32
    out = []
    for j in range(4):
        total = None
        for i in range(4):
            shift = 32 * ((i - j) % 4)
            moved = pltpu.roll(tiles[i], shift, 1) if shift else tiles[i]
            total = moved if total is None else jnp.where(quarter == i, moved, total)
        out.append(total)
    return out


def product_kernel(
    traces, taper_any, m_ref,
    tr, taper, by_s, zsend, zin, own, a_buf, b_buf, early, c_out, c_in, c_own, zret,
    t_sem, w_sem, m_sem, zs_sem, zr_sem, as_sem, ar_sem, bs_sem, br_sem, cs_sem, cr_sem, rs_sem, rr_sem,
):
    x, y, z, core = place()
    in_plane = z < FREQ
    x_half, x_core = lax.rem(x, 2), x // 2
    samples = traces.shape[-1]

    def remote(src, dst, send, recv, target):
        return pltpu.make_async_remote_copy(
            src_ref=src, dst_ref=dst, send_sem=send, recv_sem=recv, device_id=target, device_id_type=MESH
        )

    def arrived(ref, sem):
        remote(ref, ref, sem, sem, device(x, y, z, core)).wait_recv()

    def sent(ref, sem):
        remote(ref, ref, sem, sem, device(x, y, z, core)).wait_send()

    chunks = t_sem.shape[0]
    per_chunk = 16 // chunks

    def load(chunk):
        rows = pl.ds(chunk * per_chunk, per_chunk)
        return pltpu.make_async_copy(traces.at[:, rows], tr.at[:, rows], t_sem.at[chunk])

    load_taper = pltpu.make_async_copy(taper_any, taper, w_sem)
    load_taper.start()
    for chunk in range(chunks):
        load(chunk).start()

    barrier = pltpu.get_barrier_semaphore()

    def greet(target):
        pl.semaphore_signal(barrier, inc=1, device_id=target, device_id_type=MESH)

    @pl.when(in_plane)
    def _():
        for step in (8, 7, 9, 6, 10, 5, 11, 4, 12, 3, 13, 2, 14, 1, 15):
            greet(device(x, y, lax.rem(z + step, 16), core))
        for step in (2, 1, 3):
            for other in (0, 1):
                greet(device(lax.rem(x + step, 4), y, z, other))
            greet(device(x, lax.rem(y + step, 4), z, core))
        greet(device(x, y, z, 1 - core))

    rows = fourier_rows(samples)
    load_taper.wait()
    high, low = split_in_two(rows * taper[...] / math.sqrt(samples))
    weights = jnp.concatenate([high, low])
    for s in range(0, 16, 2):
        if s % per_chunk == 0:
            load(s // per_chunk).wait()
        block = jnp.concatenate([tr[:, s], tr[:, s + 1]]).reshape(256, samples)
        both = lax.dot_general(weights, block, (((1,), (1,)), ((), ())), preferred_element_type=F32)
        summed = both[:16] + both[16:]
        by_s[pl.ds(s * 16, 16)] = summed[:, :128]
        by_s[pl.ds(s * 16 + 16, 16)] = summed[:, 128:]
    for freq in range(FREQ):
        for part in range(2):
            zsend[freq, part] = by_s[pl.ds(part * FREQ + freq, 16, stride=16), :].astype(BF16)

    @pl.when(in_plane)
    def _():
        pl.semaphore_wait(barrier, 7 + 9 + 1)

    @pl.when(jnp.logical_not(in_plane))
    def _():
        pl.semaphore_wait(barrier, 8)

    others_first = (1, 7, 2, 6, 3, 5, 4)

    def to_plane(step):
        freq = lax.rem(z + step, 8)
        return remote(zsend.at[freq], zin.at[z], zs_sem, zr_sem.at[z // 4], device(x, y, freq, core))

    @pl.when(jnp.logical_not(in_plane))
    def _():
        to_plane(0).start()

    for step in others_first:
        to_plane(step).start()

    def product_of_plane():
        zin[z] = zsend[z]

        def a_copy(group, step):
            return remote(
                own.at[group], a_buf.at[x_half, group, core], as_sem.at[0 if step else 1], ar_sem.at[group // 2],
                device(lax.rem(x + step, 4), y, z, x_core),
            )

        def b_copy(group, step):
            return remote(
                own.at[group], b_buf.at[group, :, :, y], bs_sem, br_sem.at[group // 2],
                device(x, lax.rem(y + step, 4), z, core),
            )

        def arrange(group):
            @pl.when(group == z // 4)
            def _():
                arrived(zin.at[pl.ds(0, 3)], zr_sem.at[group])

            @pl.when(group != z // 4)
            def _():
                arrived(zin.at[pl.ds(0, 4)], zr_sem.at[group])

            for part in range(2):
                tiles = swap_quarters([zin[group * 4 + i, part].astype(F32) for i in range(4)])
                for j in range(4):
                    tile = tiles[j].astype(BF16)
                    rows = pl.ds(j % 2 * 16, 16)
                    own[group, part, j // 2, rows] = tile
                    b_buf[group, part, j // 2, y, rows] = tile
            for step in (2, 1, 3):
                b_copy(group, step).start()
            for step in (2, 1, 3):
                a_copy(group, step).start()

            @pl.when(x_core != core)
            def _():
                a_copy(group, 0).start()

            @pl.when(x_core == core)
            def _():
                a_buf[x_half, group, core] = own[group]

        def await_a(late):
            @pl.when(x_core == core)
            def _():
                arrived(a_buf.at[:, pl.ds(0, 3), 0], ar_sem.at[late])

            @pl.when(x_core != core)
            def _():
                arrived(a_buf.at[:, pl.ds(0, 2)], ar_sem.at[late])

        def await_b(late):
            arrived(a_buf.at[:, pl.ds(0, 3), 0], br_sem.at[late])

        def right(part, deep):
            return jnp.concatenate(
                [
                    jnp.concatenate(
                        [b_buf[2 * deep + wide, part, half].reshape(128, 128) for wide in range(2)], axis=1
                    )
                    for half in range(2)
                ]
            )

        def left(upper, deep):
            return jnp.concatenate(
                [
                    jnp.concatenate(
                        [a_buf[half, 2 * upper + deep, rows_of, part].reshape(64, 128) for half in range(2)], axis=1
                    )
                    for rows_of in (1 - core, core)
                    for part in range(2)
                ]
            )

        def multiply(upper, deep):
            rows = left(upper, deep)
            by_real = jnp.dot(rows, right(0, deep), preferred_element_type=F32)
            by_imag = jnp.dot(rows, right(1, deep), preferred_element_type=F32)
            out = []
            for at in (0, 128):
                out.append(by_real[at : at + 64] - by_imag[at + 64 : at + 128])
                out.append(by_imag[at : at + 64] + by_real[at + 64 : at + 128])
            return out

        def to_partner(upper):
            return remote(
                c_out.at[upper], c_in.at[upper], cs_sem.at[upper], cr_sem.at[upper], device(x, y, z, 1 - core)
            )

        def back(target):
            return remote(
                zret.at[target], m_ref.at[z], rs_sem, rr_sem, device(x, y, target, core)
            )

        def send_back(upper):
            for wide in range(2):
                group = 2 * upper + wide
                for part in range(2):
                    tiles = []
                    for j in range(4):
                        at = (upper, part, pl.ds(j * 16, 16), pl.ds(wide * 128, 128))
                        tiles.append(c_own[at] + c_in[at])
                    tiles = swap_quarters(tiles)
                    for i in range(4):
                        zret[group * 4 + i, part] = (tiles[i] * (1.0 / 32.0)).astype(BF16)
                for i in range(4):
                    target = group * 4 + i

                    @pl.when(target != z)
                    def _():
                        back(target).start()

        @pl.loop(0, 2)
        def _(index):
            arrange((z // 4) ^ index)

        await_a(0)
        await_b(0)
        for k, value in enumerate(multiply(0, 0)):
            early[k] = value

        @pl.loop(0, 2)
        def _(index):
            arrange(2 + (1 - z // 4) ^ index)

        await_b(1)
        values = multiply(0, 1)
        for part in range(2):
            c_out[0, part] = early[part] + values[part]
        to_partner(0).start()
        for part in range(2):
            c_own[0, part] = early[2 + part] + values[2 + part]
        to_partner(0).wait_recv()
        send_back(0)
        keep = pltpu.make_async_copy(zret.at[z], m_ref.at[z], m_sem)
        keep.start()

        await_a(1)
        values = [a + b for a, b in zip(multiply(1, 0), multiply(1, 1))]
        for part in range(2):
            c_out[1, part] = values[part]
        to_partner(1).start()
        for part in range(2):
            c_own[1, part] = values[2 + part]
        to_partner(1).wait_recv()
        send_back(1)

        keep.wait()
        to_partner(0).wait_send()
        to_partner(1).wait_send()
        sent(a_buf.at[:, pl.ds(0, 3)], as_sem.at[0])
        sent(a_buf.at[:, pl.ds(0, 3)], bs_sem)

        @pl.when(x_core != core)
        def _():
            sent(a_buf.at[0, :, 0], as_sem.at[1])

        sent(zret.at[pl.ds(0, 15)], rs_sem)

    pl.when(in_plane)(product_of_plane)

    @pl.when(in_plane)
    def _():
        sent(zsend.at[pl.ds(0, 7)], zs_sem)

    @pl.when(jnp.logical_not(in_plane))
    def _():
        sent(zsend, zs_sem)

    @pl.when(in_plane)
    def _():
        arrived(zsend.at[pl.ds(0, 7)], rr_sem)

    @pl.when(jnp.logical_not(in_plane))
    def _():
        arrived(zsend, rr_sem)


def time_kernel(m_ref, basis, out, by_cf, timed, o_sem):
    for freq in range(FREQ):
        for part in range(2):
            by_cf[pl.ds((part * FREQ + freq) * 16, 16)] = m_ref[freq, part].astype(F32)
    high, low = split_in_two(basis[...] * (1.0 / math.sqrt(FREQ)))
    weights = jnp.concatenate([high, low])
    pieces = o_sem.shape[0]
    width = 16 // pieces

    def store(piece):
        rows = pl.ds(piece * width, width)
        return pltpu.make_async_copy(timed.at[:, rows], out.at[:, rows], o_sem.at[piece])

    for piece in range(pieces):
        for s in range(piece * width, (piece + 1) * width):
            rows = by_cf[pl.ds(s, 16, stride=16), :].astype(BF16)
            rows = jnp.concatenate([rows, rows])
            values = lax.dot_general(rows, weights, (((0,), (0,)), ((), ())), preferred_element_type=F32)
            timed[:, s] = values.astype(BF16).reshape(4, 32, timed.shape[-1])
        store(piece).start()
    for piece in range(pieces):
        store(piece).wait()


def on_device(traces, taper_weights):
    shots, receivers, samples = traces.shape
    table = fourier_table(samples)
    vmem, anywhere = pl.BlockSpec(memory_space=pltpu.VMEM), pl.BlockSpec(memory_space=pl.ANY)
    dma = pltpu.SemaphoreType.DMA
    product = pl.pallas_call(
        product_kernel,
        out_shape=jax.ShapeDtypeStruct((FREQ, 2, 16, 128), BF16),
        in_specs=[anywhere, anywhere],
        out_specs=anywhere,
        scratch_shapes=[
            pltpu.VMEM((4, 16, receivers, samples), BF16),
            pltpu.VMEM((1, samples), F32),
            pltpu.VMEM((256, 128), F32),
            pltpu.VMEM((FREQ, 2, 16, 128), BF16),
            pltpu.VMEM((16, 2, 16, 128), BF16),
            pltpu.VMEM((4, 2, 2, 32, 128), BF16),
            pltpu.VMEM((2, 4, 2, 2, 2, 32, 128), BF16),
            pltpu.VMEM((4, 2, 2, 4, 32, 128), BF16),
            pltpu.VMEM((4, 64, 256), F32),
            pltpu.VMEM((2, 2, 64, 256), F32),
            pltpu.VMEM((2, 2, 64, 256), F32),
            pltpu.VMEM((2, 2, 64, 256), F32),
            pltpu.VMEM((16, 2, 16, 128), BF16),
            dma((4,)), dma, dma, dma, dma((4,)), dma((2,)), dma((2,)), dma, dma((2,)),
            dma((2,)), dma((2,)), dma, dma,
        ],
        compiler_params=pltpu.CompilerParams(
            collective_id=0, has_side_effects=True, vmem_limit_bytes=52 << 20
        ),
        name="product",
    )(traces.reshape(4, 16, receivers, samples), taper_weights.reshape(1, samples))
    timed = pl.pallas_call(
        time_kernel,
        out_shape=jax.ShapeDtypeStruct((4, 16, receivers, samples), BF16),
        in_specs=[vmem, vmem],
        out_specs=anywhere,
        scratch_shapes=[
            pltpu.VMEM((256, 128), F32),
            pltpu.VMEM((4, 16, receivers, samples), BF16),
            dma((4,)),
        ],
        compiler_params=pltpu.CompilerParams(vmem_limit_bytes=52 << 20),
        name="back_to_time",
    )(product, table)
    return timed.reshape(shots, receivers, samples)


def solution(mesh):
    placed = (P("shot", "rcv", None), P())
    return jax.shard_map(
        on_device, mesh=mesh, in_specs=placed, out_specs=P("shot", "rcv", None), check_vma=False
    )
```

```python
import functools
import math

import jax
import jax.numpy as jnp
import numpy as np
from jax import lax
from jax.experimental import pallas as pl
from jax.experimental.pallas import tpu as pltpu
from jax.sharding import PartitionSpec as P

FREQ = 8
MESH = pl.DeviceIdType.MESH
BF16, F32 = jnp.bfloat16, jnp.float32


def fourier_table(samples_count):
    samples = np.arange(samples_count)
    freq_bins = 1 + 3 * np.arange(FREQ)
    phases = 2.0 * math.pi * (freq_bins[:, None] * samples[None, :] % samples_count) / samples_count
    return np.concatenate([np.cos(phases), -np.sin(phases)]).astype(np.float32)


def fourier_rows(samples_count):
    row = lax.broadcasted_iota(jnp.int32, (2 * FREQ, samples_count), 0)
    sample = lax.broadcasted_iota(jnp.int32, (2 * FREQ, samples_count), 1)
    quarters = 1 + row // FREQ
    turns = (1 + 3 * (row % FREQ)) * sample + quarters * (samples_count // 4) + samples_count // 2
    turns = turns % samples_count - samples_count // 2
    return jnp.sin(turns.astype(F32) * (2.0 * math.pi / samples_count))


def place():
    shot, rcv = lax.axis_index("shot"), lax.axis_index("rcv")
    return lax.rem(rcv, 4), lax.rem(shot // 2, 4), shot // 8 * 8 + rcv // 4, lax.rem(shot, 2)


def device(x, y, z, core):
    return (z // 8 * 8 + y * 2 + core, lax.rem(z, 8) * 4 + x)


def ring(value, size):
    return lax.rem(value + size, size)


def split_in_two(value):
    high = value.astype(BF16)
    return high, (value - high.astype(F32)).astype(BF16)


def swap_quarters(tiles):
    quarter = lax.broadcasted_iota(jnp.int32, tiles[0].shape, 1) // 32
    out = []
    for j in range(4):
        total = None
        for i in range(4):
            shift = 32 * ((i - j) % 4)
            moved = pltpu.roll(tiles[i], shift, 1) if shift else tiles[i]
            total = moved if total is None else jnp.where(quarter == i, moved, total)
        out.append(total)
    return out


def product_kernel(
    traces, taper, m_ref,
    tr, by_s, zsend, zin, own, a_buf, b_buf, early, c_out, c_in, c_own, zret,
    t_sem, m_sem, zs_sem, zr_sem, as_sem, ar_sem, bs_sem, br_sem, cs_sem, cr_sem, rs_sem, rr_sem,
):
    x, y, z, core = place()
    in_plane = z < FREQ
    x_half, x_core = lax.rem(x, 2), x // 2
    samples = traces.shape[-1]

    def remote(src, dst, send, recv, target):
        return pltpu.make_async_remote_copy(
            src_ref=src, dst_ref=dst, send_sem=send, recv_sem=recv, device_id=target, device_id_type=MESH
        )

    def arrived(ref, sem):
        remote(ref, ref, sem, sem, device(x, y, z, core)).wait_recv()

    def sent(ref, sem):
        remote(ref, ref, sem, sem, device(x, y, z, core)).wait_send()

    chunks = t_sem.shape[0]
    per_chunk = 16 // chunks

    def load(chunk):
        rows = pl.ds(chunk * per_chunk, per_chunk)
        return pltpu.make_async_copy(traces.at[:, rows], tr.at[:, rows], t_sem.at[chunk])

    for chunk in range(chunks):
        load(chunk).start()

    barrier = pltpu.get_barrier_semaphore()

    def greet(target):
        pl.semaphore_signal(barrier, inc=1, device_id=target, device_id_type=MESH)

    @pl.when(in_plane)
    def _():
        for step in (8, 7, 9, 6, 10, 5, 11, 4, 12, 3, 13, 2, 14, 1, 15):
            greet(device(x, y, lax.rem(z + step, 16), core))
        for step in (2, 1, 3):
            for other in (0, 1):
                greet(device(lax.rem(x + step, 4), y, z, other))
            greet(device(x, lax.rem(y + step, 4), z, core))
        greet(device(x, y, z, 1 - core))

    high, low = split_in_two(fourier_rows(samples) * taper[...] / math.sqrt(samples))
    weights = jnp.concatenate([high, low])
    for s in range(0, 16, 2):
        if s % per_chunk == 0:
            load(s // per_chunk).wait()
        block = jnp.concatenate([tr[:, s], tr[:, s + 1]]).reshape(256, samples)
        both = lax.dot_general(weights, block, (((1,), (1,)), ((), ())), preferred_element_type=F32)
        summed = both[:16] + both[16:]
        by_s[pl.ds(s * 16, 16)] = summed[:, :128]
        by_s[pl.ds(s * 16 + 16, 16)] = summed[:, 128:]
    for freq in range(FREQ):
        for part in range(2):
            zsend[freq, part] = by_s[pl.ds(part * FREQ + freq, 16, stride=16), :].astype(BF16)

    @pl.when(in_plane)
    def _():
        pl.semaphore_wait(barrier, 7 + 9 + 1)

    @pl.when(jnp.logical_not(in_plane))
    def _():
        pl.semaphore_wait(barrier, 8)

    def to_plane(freq):
        return remote(zsend.at[freq], zin.at[z], zs_sem, zr_sem.at[z // 4], device(x, y, freq, core))

    last_started = jnp.logical_and(z >= 8, z < 12)

    @pl.when(last_started)
    def _():
        for freq in reversed(range(FREQ)):
            to_plane(freq).start()

    @pl.when(jnp.logical_not(last_started))
    def _():
        for freq in range(FREQ):

            @pl.when(freq != z)
            def _():
                to_plane(freq).start()

    def product_of_plane():
        zin[z] = zsend[z]

        def a_copy(group, step):
            return remote(
                own.at[group], a_buf.at[x_half, group, core], as_sem.at[0 if step else 1], ar_sem.at[group // 2],
                device(lax.rem(x + step, 4), y, z, x_core),
            )

        def b_copy(group, step):
            return remote(
                own.at[group], b_buf.at[group, :, :, y], bs_sem, br_sem.at[jnp.maximum(group - 1, 0)],
                device(x, lax.rem(y + step, 4), z, core),
            )

        def arrange(group):
            @pl.when(group == z // 4)
            def _():
                arrived(zin.at[pl.ds(0, 3)], zr_sem.at[group])

            @pl.when(group != z // 4)
            def _():
                arrived(zin.at[pl.ds(0, 4)], zr_sem.at[group])

            for part in range(2):
                tiles = swap_quarters([zin[group * 4 + i, part].astype(F32) for i in range(4)])
                for j in range(4):
                    tile = tiles[j].astype(BF16)
                    rows = pl.ds(j % 2 * 16, 16)
                    own[group, part, j // 2, rows] = tile
                    b_buf[group, part, j // 2, y, rows] = tile
            for step in (2, 1, 3):
                b_copy(group, step).start()
            for step in (2, 1, 3):
                a_copy(group, step).start()

            @pl.when(x_core != core)
            def _():
                a_copy(group, 0).start()

            @pl.when(x_core == core)
            def _():
                a_buf[x_half, group, core] = own[group]

        def await_a(late):
            @pl.when(x_core == core)
            def _():
                arrived(a_buf.at[:, pl.ds(0, 3), 0], ar_sem.at[late])

            @pl.when(x_core != core)
            def _():
                arrived(a_buf.at[:, pl.ds(0, 2)], ar_sem.at[late])

        def await_b(part, pieces):
            arrived(a_buf.at[0 : pieces // 3, pl.ds(0, 3), 0], br_sem.at[part])

        def right(deep, wide):
            return jnp.concatenate(
                [
                    jnp.concatenate([b_buf[2 * deep + wide, part, half].reshape(128, 128) for part in range(2)], axis=1)
                    for half in range(2)
                ]
            )

        def left(upper, deep):
            return jnp.concatenate(
                [
                    jnp.concatenate(
                        [a_buf[half, 2 * upper + deep, rows_of, part].reshape(64, 128) for half in range(2)], axis=1
                    )
                    for rows_of in (1 - core, core)
                    for part in range(2)
                ]
            )

        def multiply(upper, deep, wide):
            both = jnp.dot(left(upper, deep), right(deep, wide), preferred_element_type=F32)
            by_real, by_imag = both[:, :128], both[:, 128:]
            out = []
            for at in (0, 128):
                out.append(by_real[at : at + 64] - by_imag[at + 64 : at + 128])
                out.append(by_imag[at : at + 64] + by_real[at + 64 : at + 128])
            return out

        def to_partner(upper, wide):
            return remote(
                c_out.at[upper, wide], c_in.at[upper, wide], cs_sem, cr_sem.at[upper, wide], device(x, y, z, 1 - core)
            )

        def back(target):
            return remote(zret.at[target], m_ref.at[z], rs_sem, rr_sem, device(x, y, target, core))

        def send_back(upper, wide):
            arrived(c_in.at[upper, wide], cr_sem.at[upper, wide])
            group = 2 * upper + wide
            for part in range(2):
                tiles = []
                for j in range(4):
                    at = (upper, wide, part, pl.ds(j * 16, 16))
                    tiles.append(c_own[at] + c_in[at])
                tiles = swap_quarters(tiles)
                for i in range(4):
                    zret[group * 4 + i, part] = (tiles[i] * (1.0 / 32.0)).astype(BF16)
            for i in range(4):
                target = group * 4 + i

                @pl.when(target != z)
                def _():
                    back(target).start()

        def add_up(upper, wide, first, second):
            for part in range(2):
                c_out[upper, wide, part] = first[part] + second[part]
            to_partner(upper, wide).start()
            for part in range(2):
                c_own[upper, wide, part] = first[2 + part] + second[2 + part]

        def group_at(index):
            near = jnp.where(z < 4, 3, 2)
            return jnp.where(index < 2, (z // 4) ^ index, jnp.where(index == 2, near, 5 - near))

        @pl.loop(0, 2)
        def _(index):
            arrange(group_at(index))

        await_a(0)
        await_b(0, 6)
        for wide in range(2):
            for k, value in enumerate(multiply(0, 0, wide)):
                early[wide, k] = value

        @pl.loop(2, 4)
        def _(index):
            arrange(group_at(index))

        await_b(1, 3)
        add_up(0, 0, early[0], multiply(0, 1, 0))
        await_b(2, 3)
        add_up(0, 1, early[1], multiply(0, 1, 1))
        send_back(0, 0)
        await_a(1)
        add_up(1, 1, multiply(1, 0, 1), multiply(1, 1, 1))
        send_back(0, 1)
        keep = pltpu.make_async_copy(zret.at[z], m_ref.at[z], m_sem)
        keep.start()
        add_up(1, 0, multiply(1, 0, 0), multiply(1, 1, 0))
        send_back(1, 1)
        send_back(1, 0)

        keep.wait()
        sent(c_out, cs_sem)
        sent(a_buf.at[:, pl.ds(0, 3)], as_sem.at[0])
        sent(a_buf.at[:, pl.ds(0, 3)], bs_sem)

        @pl.when(x_core != core)
        def _():
            sent(a_buf.at[0, :, 0], as_sem.at[1])

        sent(zret.at[pl.ds(0, 15)], rs_sem)

    pl.when(in_plane)(product_of_plane)

    @pl.when(in_plane)
    def _():
        sent(zsend.at[pl.ds(0, 7)], zs_sem)

    @pl.when(jnp.logical_not(in_plane))
    def _():
        sent(zsend, zs_sem)

    @pl.when(in_plane)
    def _():
        arrived(zsend.at[pl.ds(0, 7)], rr_sem)

    @pl.when(jnp.logical_not(in_plane))
    def _():
        arrived(zsend, rr_sem)


def time_kernel(m_ref, basis, out, by_cf, timed, o_sem):
    for freq in range(FREQ):
        for part in range(2):
            by_cf[pl.ds((part * FREQ + freq) * 16, 16)] = m_ref[freq, part].astype(F32)
    high, low = split_in_two(basis[...] * (1.0 / math.sqrt(FREQ)))
    weights = jnp.concatenate([high, low])
    pieces = o_sem.shape[0]
    width = 16 // pieces

    def store(piece):
        rows = pl.ds(piece * width, width)
        return pltpu.make_async_copy(timed.at[:, rows], out.at[:, rows], o_sem.at[piece])

    for piece in range(pieces):
        for s in range(piece * width, (piece + 1) * width):
            rows = by_cf[pl.ds(s, 16, stride=16), :].astype(BF16)
            rows = jnp.concatenate([rows, rows])
            values = lax.dot_general(rows, weights, (((0,), (0,)), ((), ())), preferred_element_type=F32)
            timed[:, s] = values.astype(BF16).reshape(4, 32, timed.shape[-1])
        store(piece).start()
    for piece in range(pieces):
        store(piece).wait()


def on_device(traces, taper_weights):
    shots, receivers, samples = traces.shape
    table = fourier_table(samples)
    vmem, anywhere = pl.BlockSpec(memory_space=pltpu.VMEM), pl.BlockSpec(memory_space=pl.ANY)
    dma = pltpu.SemaphoreType.DMA
    product = pl.pallas_call(
        product_kernel,
        out_shape=jax.ShapeDtypeStruct((FREQ, 2, 16, 128), BF16),
        in_specs=[anywhere, vmem],
        out_specs=anywhere,
        scratch_shapes=[
            pltpu.VMEM((4, 16, receivers, samples), BF16),
            pltpu.VMEM((256, 128), F32),
            pltpu.VMEM((FREQ, 2, 16, 128), BF16),
            pltpu.VMEM((16, 2, 16, 128), BF16),
            pltpu.VMEM((4, 2, 2, 32, 128), BF16),
            pltpu.VMEM((2, 4, 2, 2, 2, 32, 128), BF16),
            pltpu.VMEM((4, 2, 2, 4, 32, 128), BF16),
            pltpu.VMEM((2, 4, 64, 128), F32),
            pltpu.VMEM((2, 2, 2, 64, 128), F32),
            pltpu.VMEM((2, 2, 2, 64, 128), F32),
            pltpu.VMEM((2, 2, 2, 64, 128), F32),
            pltpu.VMEM((16, 2, 16, 128), BF16),
            dma((4,)), dma, dma, dma((4,)), dma((2,)), dma((2,)), dma, dma((3,)),
            dma, dma((2, 2)), dma, dma,
        ],
        compiler_params=pltpu.CompilerParams(
            collective_id=0, has_side_effects=True, vmem_limit_bytes=52 << 20
        ),
        name="product",
    )(traces.reshape(4, 16, receivers, samples), taper_weights.reshape(1, samples))
    timed = pl.pallas_call(
        time_kernel,
        out_shape=jax.ShapeDtypeStruct((4, 16, receivers, samples), BF16),
        in_specs=[vmem, vmem],
        out_specs=anywhere,
        scratch_shapes=[
            pltpu.VMEM((256, 128), F32),
            pltpu.VMEM((4, 16, receivers, samples), BF16),
            dma((4,)),
        ],
        compiler_params=pltpu.CompilerParams(vmem_limit_bytes=52 << 20),
        name="back_to_time",
    )(product, table)
    return timed.reshape(shots, receivers, samples)


def solution(mesh):
    placed = (P("shot", "rcv", None), P())
    return jax.shard_map(
        on_device, mesh=mesh, in_specs=placed, out_specs=P("shot", "rcv", None), check_vma=False
    )
```

```python
import functools
import math

import jax
import jax.numpy as jnp
import numpy as np
from jax import lax
from jax.experimental import pallas as pl
from jax.experimental.pallas import tpu as pltpu
from jax.sharding import PartitionSpec as P

FREQ = 8
MESH = pl.DeviceIdType.MESH
BF16, F32 = jnp.bfloat16, jnp.float32


def fourier_table(samples_count):
    samples = np.arange(samples_count)
    freq_bins = 1 + 3 * np.arange(FREQ)
    phases = 2.0 * math.pi * (freq_bins[:, None] * samples[None, :] % samples_count) / samples_count
    return np.concatenate([np.cos(phases), -np.sin(phases)]).astype(np.float32)


def fourier_rows(samples_count):
    row = lax.broadcasted_iota(jnp.int32, (2 * FREQ, samples_count), 0)
    sample = lax.broadcasted_iota(jnp.int32, (2 * FREQ, samples_count), 1)
    quarters = 1 + row // FREQ
    turns = (1 + 3 * (row % FREQ)) * sample + quarters * (samples_count // 4) + samples_count // 2
    turns = turns % samples_count - samples_count // 2
    return jnp.sin(turns.astype(F32) * (2.0 * math.pi / samples_count))


def place():
    shot, rcv = lax.axis_index("shot"), lax.axis_index("rcv")
    return lax.rem(rcv, 4), lax.rem(shot // 2, 4), shot // 8 * 8 + rcv // 4, lax.rem(shot, 2)


def device(x, y, z, core):
    return (z // 8 * 8 + y * 2 + core, lax.rem(z, 8) * 4 + x)


def ring(value, size):
    return lax.rem(value + size, size)


def split_in_two(value):
    high = value.astype(BF16)
    return high, (value - high.astype(F32)).astype(BF16)


def swap_quarters(tiles):
    quarter = lax.broadcasted_iota(jnp.int32, tiles[0].shape, 1) // 32
    out = []
    for j in range(4):
        total = None
        for i in range(4):
            shift = 32 * ((i - j) % 4)
            moved = pltpu.roll(tiles[i], shift, 1) if shift else tiles[i]
            total = moved if total is None else jnp.where(quarter == i, moved, total)
        out.append(total)
    return out


def product_kernel(
    traces, taper, m_ref,
    tr, by_s, zsend, zin, own, a_buf, b_buf, c_out, c_in, c_own, zret,
    t_sem, m_sem, zs_sem, zr_sem, as_sem, ar_sem, bs_sem, br_sem, cs_sem, cr_sem, rs_sem, rr_sem,
):
    x, y, z, core = place()
    in_plane = z < FREQ
    x_half, x_core = lax.rem(x, 2), x // 2
    samples = traces.shape[-1]

    def remote(src, dst, send, recv, target):
        return pltpu.make_async_remote_copy(
            src_ref=src, dst_ref=dst, send_sem=send, recv_sem=recv, device_id=target, device_id_type=MESH
        )

    def arrived(ref, sem):
        remote(ref, ref, sem, sem, device(x, y, z, core)).wait_recv()

    def sent(ref, sem):
        remote(ref, ref, sem, sem, device(x, y, z, core)).wait_send()

    chunks = t_sem.shape[0]
    per_chunk = 16 // chunks

    def load(chunk):
        rows = pl.ds(chunk * per_chunk, per_chunk)
        return pltpu.make_async_copy(traces.at[:, rows], tr.at[:, rows], t_sem.at[chunk])

    for chunk in range(chunks):
        load(chunk).start()

    barrier = pltpu.get_barrier_semaphore()

    def greet(target):
        pl.semaphore_signal(barrier, inc=1, device_id=target, device_id_type=MESH)

    @pl.when(in_plane)
    def _():
        for step in (8, 7, 9, 6, 10, 5, 11, 4, 12, 3, 13, 2, 14, 1, 15):
            greet(device(x, y, lax.rem(z + step, 16), core))
        for step in (2, 1, 3):
            for other in (0, 1):
                greet(device(lax.rem(x + step, 4), y, z, other))
            greet(device(x, lax.rem(y + step, 4), z, core))
        greet(device(x, y, z, 1 - core))

    high, low = split_in_two(fourier_rows(samples) * taper[...] / math.sqrt(samples))
    weights = jnp.concatenate([high, low])
    for s in range(0, 16, 2):
        if s % per_chunk == 0:
            load(s // per_chunk).wait()
        block = jnp.concatenate([tr[:, s], tr[:, s + 1]]).reshape(256, samples)
        both = lax.dot_general(weights, block, (((1,), (1,)), ((), ())), preferred_element_type=F32)
        summed = both[:16] + both[16:]
        by_s[pl.ds(s * 16, 16)] = summed[:, :128]
        by_s[pl.ds(s * 16 + 16, 16)] = summed[:, 128:]
    for freq in range(FREQ):
        for part in range(2):
            zsend[freq, part] = by_s[pl.ds(part * FREQ + freq, 16, stride=16), :].astype(BF16)

    @pl.when(in_plane)
    def _():
        pl.semaphore_wait(barrier, 7 + 9 + 1)

    @pl.when(jnp.logical_not(in_plane))
    def _():
        pl.semaphore_wait(barrier, 8)

    def to_plane(freq):
        return remote(zsend.at[freq], zin.at[z], zs_sem, zr_sem.at[z // 4], device(x, y, freq, core))

    last_started = jnp.logical_and(z >= 8, z < 12)

    @pl.when(last_started)
    def _():
        for freq in reversed(range(FREQ)):
            to_plane(freq).start()

    @pl.when(jnp.logical_not(last_started))
    def _():
        for freq in range(FREQ):

            @pl.when(freq != z)
            def _():
                to_plane(freq).start()

    def product_of_plane():
        zin[z] = zsend[z]

        def a_copy(group, step):
            return remote(
                own.at[group], a_buf.at[x_half, group, core], as_sem.at[0 if step else 1], ar_sem.at[group // 2],
                device(lax.rem(x + step, 4), y, z, x_core),
            )

        def b_copy(group, step):
            return remote(
                own.at[group], b_buf.at[group, :, :, y], bs_sem, br_sem.at[group],
                device(x, lax.rem(y + step, 4), z, core),
            )

        def arrange(group):
            @pl.when(group == z // 4)
            def _():
                arrived(zin.at[pl.ds(0, 3)], zr_sem.at[group])

            @pl.when(group != z // 4)
            def _():
                arrived(zin.at[pl.ds(0, 4)], zr_sem.at[group])

            for part in range(2):
                tiles = swap_quarters([zin[group * 4 + i, part].astype(F32) for i in range(4)])
                for j in range(4):
                    tile = tiles[j].astype(BF16)
                    rows = pl.ds(j % 2 * 16, 16)
                    own[group, part, j // 2, rows] = tile
                    b_buf[group, part, j // 2, y, rows] = tile
        def send_a(group):
            for step in (2, 1, 3):
                a_copy(group, step).start()

            @pl.when(x_core != core)
            def _():
                a_copy(group, 0).start()

            @pl.when(x_core == core)
            def _():
                a_buf[x_half, group, core] = own[group]

        def send_b(group):
            for step in (2, 1, 3):
                b_copy(group, step).start()

        def await_a(late):
            @pl.when(x_core == core)
            def _():
                arrived(a_buf.at[:, pl.ds(0, 3), 0], ar_sem.at[late])

            @pl.when(x_core != core)
            def _():
                arrived(a_buf.at[:, pl.ds(0, 2)], ar_sem.at[late])

        def await_b(group):
            arrived(a_buf.at[0, pl.ds(0, 3), 0], br_sem.at[group])

        def right(deep, wide):
            return jnp.concatenate(
                [
                    jnp.concatenate([b_buf[2 * deep + wide, part, half].reshape(128, 128) for part in range(2)], axis=1)
                    for half in range(2)
                ]
            )

        def left(upper, deep):
            return jnp.concatenate(
                [
                    jnp.concatenate(
                        [a_buf[half, 2 * upper + deep, rows_of, part].reshape(64, 128) for half in range(2)], axis=1
                    )
                    for rows_of in (1 - core, core)
                    for part in range(2)
                ]
            )

        def multiply(upper, deep, wide):
            both = jnp.dot(left(upper, deep), right(deep, wide), preferred_element_type=F32)
            by_real, by_imag = both[:, :128], both[:, 128:]
            out = []
            for at in (0, 128):
                out.append(by_real[at : at + 64] - by_imag[at + 64 : at + 128])
                out.append(by_imag[at : at + 64] + by_real[at + 64 : at + 128])
            return out

        def to_partner(upper, wide):
            return remote(
                c_out.at[upper, wide], c_in.at[upper, wide], cs_sem, cr_sem.at[upper, wide], device(x, y, z, 1 - core)
            )

        def back(target):
            return remote(zret.at[target], m_ref.at[z], rs_sem, rr_sem, device(x, y, target, core))

        def send_back(upper, wide):
            arrived(c_in.at[upper, wide], cr_sem.at[upper, wide])
            group = 2 * upper + wide
            for part in range(2):
                tiles = []
                for j in range(4):
                    at = (upper, wide, part, pl.ds(j * 16, 16))
                    tiles.append(c_own[at] + c_in[at])
                tiles = swap_quarters(tiles)
                for i in range(4):
                    zret[group * 4 + i, part] = (tiles[i] * (1.0 / 32.0)).astype(BF16)
            for i in range(4):
                target = group * 4 + i

                @pl.when(target != z)
                def _():
                    back(target).start()

        def add_up(upper, wide, first, second):
            for part in range(2):
                c_out[upper, wide, part] = first[part] + second[part]
            to_partner(upper, wide).start()
            for part in range(2):
                c_own[upper, wide, part] = first[2 + part] + second[2 + part]

        def group_at(index):
            near = 2
            return jnp.where(index < 2, (z // 4) ^ index, jnp.where(index == 2, near, 5 - near))

        @pl.loop(0, 2)
        def _(index):
            group = group_at(index)
            arrange(group)

            @pl.when(group == 0)
            def _():
                send_b(group)

            send_a(group)

        @pl.loop(2, 4)
        def _(index):
            group = group_at(index)
            arrange(group)

            @pl.when(group == 2)
            def _():
                send_b(group)

        for group in (2, 3):
            send_a(group)
        for group in (1, 3):
            send_b(group)

        await_a(0)
        await_b(0)
        await_b(2)
        add_up(0, 0, multiply(0, 0, 0), multiply(0, 1, 0))
        send_back(0, 0)
        await_a(1)
        add_up(1, 0, multiply(1, 0, 0), multiply(1, 1, 0))
        await_b(1)
        await_b(3)
        add_up(1, 1, multiply(1, 0, 1), multiply(1, 1, 1))
        send_back(1, 0)
        add_up(0, 1, multiply(0, 0, 1), multiply(0, 1, 1))
        send_back(1, 1)
        send_back(0, 1)
        keep = pltpu.make_async_copy(zret.at[z], m_ref.at[z], m_sem)
        keep.start()

        keep.wait()
        sent(c_out, cs_sem)
        sent(a_buf.at[:, pl.ds(0, 3)], as_sem.at[0])
        sent(a_buf.at[:, pl.ds(0, 3)], bs_sem)

        @pl.when(x_core != core)
        def _():
            sent(a_buf.at[0, :, 0], as_sem.at[1])

        sent(zret.at[pl.ds(0, 15)], rs_sem)

    pl.when(in_plane)(product_of_plane)

    @pl.when(in_plane)
    def _():
        sent(zsend.at[pl.ds(0, 7)], zs_sem)

    @pl.when(jnp.logical_not(in_plane))
    def _():
        sent(zsend, zs_sem)

    @pl.when(in_plane)
    def _():
        arrived(zsend.at[pl.ds(0, 7)], rr_sem)

    @pl.when(jnp.logical_not(in_plane))
    def _():
        arrived(zsend, rr_sem)


def time_kernel(m_ref, basis, out, by_cf, timed, o_sem):
    for freq in range(FREQ):
        for part in range(2):
            by_cf[pl.ds((part * FREQ + freq) * 16, 16)] = m_ref[freq, part].astype(F32)
    high, low = split_in_two(basis[...] * (1.0 / math.sqrt(FREQ)))
    weights = jnp.concatenate([high, low])
    pieces = o_sem.shape[0]
    width = 16 // pieces

    def store(piece):
        rows = pl.ds(piece * width, width)
        return pltpu.make_async_copy(timed.at[:, rows], out.at[:, rows], o_sem.at[piece])

    for piece in range(pieces):
        for s in range(piece * width, (piece + 1) * width):
            rows = by_cf[pl.ds(s, 16, stride=16), :].astype(BF16)
            rows = jnp.concatenate([rows, rows])
            values = lax.dot_general(rows, weights, (((0,), (0,)), ((), ())), preferred_element_type=F32)
            timed[:, s] = values.astype(BF16).reshape(4, 32, timed.shape[-1])
        store(piece).start()
    for piece in range(pieces):
        store(piece).wait()


def on_device(traces, taper_weights):
    shots, receivers, samples = traces.shape
    table = fourier_table(samples)
    vmem, anywhere = pl.BlockSpec(memory_space=pltpu.VMEM), pl.BlockSpec(memory_space=pl.ANY)
    dma = pltpu.SemaphoreType.DMA
    product = pl.pallas_call(
        product_kernel,
        out_shape=jax.ShapeDtypeStruct((FREQ, 2, 16, 128), BF16),
        in_specs=[anywhere, vmem],
        out_specs=anywhere,
        scratch_shapes=[
            pltpu.VMEM((4, 16, receivers, samples), BF16),
            pltpu.VMEM((256, 128), F32),
            pltpu.VMEM((FREQ, 2, 16, 128), BF16),
            pltpu.VMEM((16, 2, 16, 128), BF16),
            pltpu.VMEM((4, 2, 2, 32, 128), BF16),
            pltpu.VMEM((2, 4, 2, 2, 2, 32, 128), BF16),
            pltpu.VMEM((4, 2, 2, 4, 32, 128), BF16),
            pltpu.VMEM((2, 2, 2, 64, 128), F32),
            pltpu.VMEM((2, 2, 2, 64, 128), F32),
            pltpu.VMEM((2, 2, 2, 64, 128), F32),
            pltpu.VMEM((16, 2, 16, 128), BF16),
            dma((4,)), dma, dma, dma((4,)), dma((2,)), dma((2,)), dma, dma((4,)),
            dma, dma((2, 2)), dma, dma,
        ],
        compiler_params=pltpu.CompilerParams(
            collective_id=0, has_side_effects=True, vmem_limit_bytes=52 << 20
        ),
        name="product",
    )(traces.reshape(4, 16, receivers, samples), taper_weights.reshape(1, samples))
    timed = pl.pallas_call(
        time_kernel,
        out_shape=jax.ShapeDtypeStruct((4, 16, receivers, samples), BF16),
        in_specs=[vmem, vmem],
        out_specs=anywhere,
        scratch_shapes=[
            pltpu.VMEM((256, 128), F32),
            pltpu.VMEM((4, 16, receivers, samples), BF16),
            dma((4,)),
        ],
        compiler_params=pltpu.CompilerParams(vmem_limit_bytes=52 << 20),
        name="back_to_time",
    )(product, table)
    return timed.reshape(shots, receivers, samples)


def solution(mesh):
    placed = (P("shot", "rcv", None), P())
    return jax.shard_map(
        on_device, mesh=mesh, in_specs=placed, out_specs=P("shot", "rcv", None), check_vma=False
    )
```

```python
import functools
import math

import jax
import jax.numpy as jnp
import numpy as np
from jax import lax
from jax.experimental import pallas as pl
from jax.experimental.pallas import tpu as pltpu
from jax.sharding import PartitionSpec as P

FREQ = 8
MESH = pl.DeviceIdType.MESH
BF16, F32 = jnp.bfloat16, jnp.float32


def fourier_table(samples_count):
    samples = np.arange(samples_count)
    freq_bins = 1 + 3 * np.arange(FREQ)
    phases = 2.0 * math.pi * (freq_bins[:, None] * samples[None, :] % samples_count) / samples_count
    return np.concatenate([np.cos(phases), -np.sin(phases)]).astype(np.float32)


def fourier_rows(samples_count):
    row = lax.broadcasted_iota(jnp.int32, (2 * FREQ, samples_count), 0)
    sample = lax.broadcasted_iota(jnp.int32, (2 * FREQ, samples_count), 1)
    quarters = 1 + row // FREQ
    turns = (1 + 3 * (row % FREQ)) * sample + quarters * (samples_count // 4) + samples_count // 2
    turns = turns % samples_count - samples_count // 2
    return jnp.sin(turns.astype(F32) * (2.0 * math.pi / samples_count))


def place():
    shot, rcv = lax.axis_index("shot"), lax.axis_index("rcv")
    return lax.rem(rcv, 4), lax.rem(shot // 2, 4), shot // 8 * 8 + rcv // 4, lax.rem(shot, 2)


def device(x, y, z, core):
    return (z // 8 * 8 + y * 2 + core, lax.rem(z, 8) * 4 + x)


def ring(value, size):
    return lax.rem(value + size, size)


def split_in_two(value):
    high = value.astype(BF16)
    return high, (value - high.astype(F32)).astype(BF16)


def swap_quarters(tiles):
    quarter = lax.broadcasted_iota(jnp.int32, tiles[0].shape, 1) // 32
    out = []
    for j in range(4):
        total = None
        for i in range(4):
            shift = 32 * ((i - j) % 4)
            moved = pltpu.roll(tiles[i], shift, 1) if shift else tiles[i]
            total = moved if total is None else jnp.where(quarter == i, moved, total)
        out.append(total)
    return out


def product_kernel(
    traces, taper, m_ref,
    tr, by_s, zsend, zin, own, a_buf, b_buf, c_out, c_in, c_own, zret,
    t_sem, m_sem, zs_sem, zr_sem, as_sem, ar_sem, bs_sem, br_sem, cs_sem, cr_sem, rs_sem, rr_sem,
):
    x, y, z, core = place()
    in_plane = z < FREQ
    x_half, x_core = lax.rem(x, 2), x // 2
    samples = traces.shape[-1]

    def remote(src, dst, send, recv, target):
        return pltpu.make_async_remote_copy(
            src_ref=src, dst_ref=dst, send_sem=send, recv_sem=recv, device_id=target, device_id_type=MESH
        )

    def arrived(ref, sem):
        remote(ref, ref, sem, sem, device(x, y, z, core)).wait_recv()

    def sent(ref, sem):
        remote(ref, ref, sem, sem, device(x, y, z, core)).wait_send()

    chunks = t_sem.shape[0]
    per_chunk = 16 // chunks

    def load(chunk):
        rows = pl.ds(chunk * per_chunk, per_chunk)
        return pltpu.make_async_copy(traces.at[:, rows], tr.at[:, rows], t_sem.at[chunk])

    for chunk in range(chunks):
        load(chunk).start()

    barrier = pltpu.get_barrier_semaphore()

    def greet(target):
        pl.semaphore_signal(barrier, inc=1, device_id=target, device_id_type=MESH)

    @pl.when(in_plane)
    def _():
        for step in (8, 7, 9, 6, 10, 5, 11, 4, 12, 3, 13, 2, 14, 1, 15):
            greet(device(x, y, lax.rem(z + step, 16), core))
        for step in (2, 1, 3):
            for other in (0, 1):
                greet(device(lax.rem(x + step, 4), y, z, other))
            greet(device(x, lax.rem(y + step, 4), z, core))
        greet(device(x, y, z, 1 - core))

    high, low = split_in_two(fourier_rows(samples) * taper[...] / math.sqrt(samples))
    weights = jnp.concatenate([high, low])
    for s in range(0, 16, 2):
        if s % per_chunk == 0:
            load(s // per_chunk).wait()
        block = jnp.concatenate([tr[:, s], tr[:, s + 1]]).reshape(256, samples)
        both = lax.dot_general(weights, block, (((1,), (1,)), ((), ())), preferred_element_type=F32)
        summed = both[:16] + both[16:]
        by_s[pl.ds(s * 16, 16)] = summed[:, :128]
        by_s[pl.ds(s * 16 + 16, 16)] = summed[:, 128:]
    for freq in range(FREQ):
        for part in range(2):
            zsend[freq, part] = by_s[pl.ds(part * FREQ + freq, 16, stride=16), :].astype(BF16)

    @pl.when(in_plane)
    def _():
        pl.semaphore_wait(barrier, 7 + 9 + 1)

    @pl.when(jnp.logical_not(in_plane))
    def _():
        pl.semaphore_wait(barrier, 8)

    def to_plane(freq):
        return remote(zsend.at[freq], zin.at[z], zs_sem, zr_sem.at[z // 4], device(x, y, freq, core))

    for freq in range(FREQ):

        @pl.when(freq != z)
        def _():
            to_plane(freq).start()

    def product_of_plane():
        zin[z] = zsend[z]

        def a_copy(group, step):
            return remote(
                own.at[group], a_buf.at[x_half, group, core], as_sem.at[0 if step else 1], ar_sem.at[group // 2],
                device(lax.rem(x + step, 4), y, z, x_core),
            )

        def b_copy(group, step):
            return remote(
                own.at[group], b_buf.at[group, :, :, y], bs_sem, br_sem.at[group],
                device(x, lax.rem(y + step, 4), z, core),
            )

        def arrange(group):
            @pl.when(group == z // 4)
            def _():
                arrived(zin.at[pl.ds(0, 3)], zr_sem.at[group])

            @pl.when(group != z // 4)
            def _():
                arrived(zin.at[pl.ds(0, 4)], zr_sem.at[group])

            for part in range(2):
                tiles = swap_quarters([zin[group * 4 + i, part].astype(F32) for i in range(4)])
                for j in range(4):
                    tile = tiles[j].astype(BF16)
                    rows = pl.ds(j % 2 * 16, 16)
                    own[group, part, j // 2, rows] = tile
                    b_buf[group, part, j // 2, y, rows] = tile
        def send_a(group):
            for step in (2, 1, 3):
                a_copy(group, step).start()

            @pl.when(x_core != core)
            def _():
                a_copy(group, 0).start()

            @pl.when(x_core == core)
            def _():
                a_buf[x_half, group, core] = own[group]

        def send_b(group):
            for step in (2, 1, 3):
                b_copy(group, step).start()

        def await_a(late):
            @pl.when(x_core == core)
            def _():
                arrived(a_buf.at[:, pl.ds(0, 3), 0], ar_sem.at[late])

            @pl.when(x_core != core)
            def _():
                arrived(a_buf.at[:, pl.ds(0, 2)], ar_sem.at[late])

        def await_b(group):
            arrived(a_buf.at[0, pl.ds(0, 3), 0], br_sem.at[group])

        def right(deep, wide):
            return jnp.concatenate(
                [
                    jnp.concatenate([b_buf[2 * deep + wide, part, half].reshape(128, 128) for part in range(2)], axis=1)
                    for half in range(2)
                ]
            )

        def left(upper, deep):
            return jnp.concatenate(
                [
                    jnp.concatenate(
                        [a_buf[half, 2 * upper + deep, rows_of, part].reshape(64, 128) for half in range(2)], axis=1
                    )
                    for rows_of in (1 - core, core)
                    for part in range(2)
                ]
            )

        def multiply(upper, deep, wide):
            both = jnp.dot(left(upper, deep), right(deep, wide), preferred_element_type=F32)
            by_real, by_imag = both[:, :128], both[:, 128:]
            out = []
            for at in (0, 128):
                out.append(by_real[at : at + 64] - by_imag[at + 64 : at + 128])
                out.append(by_imag[at : at + 64] + by_real[at + 64 : at + 128])
            return out

        def to_partner(upper, wide):
            return remote(
                c_out.at[upper, wide], c_in.at[upper, wide], cs_sem, cr_sem.at[upper, wide], device(x, y, z, 1 - core)
            )

        def back(target):
            return remote(zret.at[target], m_ref.at[z], rs_sem, rr_sem, device(x, y, target, core))

        def send_back(upper, wide):
            arrived(c_in.at[upper, wide], cr_sem.at[upper, wide])
            group = 2 * upper + wide
            for part in range(2):
                tiles = []
                for j in range(4):
                    at = (upper, wide, part, pl.ds(j * 16, 16))
                    tiles.append(c_own[at] + c_in[at])
                tiles = swap_quarters(tiles)
                for i in range(4):
                    zret[group * 4 + i, part] = (tiles[i] * (1.0 / 32.0)).astype(BF16)
            for i in range(4):
                target = group * 4 + i

                @pl.when(target != z)
                def _():
                    back(target).start()

        def add_up(upper, wide, first, second):
            for part in range(2):
                c_out[upper, wide, part] = first[part] + second[part]
            to_partner(upper, wide).start()
            for part in range(2):
                c_own[upper, wide, part] = first[2 + part] + second[2 + part]

        @pl.loop(0, 2)
        def _(index):
            group = (z // 4) ^ index
            arrange(group)

            @pl.when(group == 0)
            def _():
                send_b(group)

            send_a(group)

        arrange(2)
        send_b(2)
        send_a(2)
        send_b(1)
        arrange(3)
        send_a(3)
        send_b(3)

        await_a(0)
        await_b(0)
        await_b(2)
        add_up(0, 0, multiply(0, 0, 0), multiply(0, 1, 0))
        send_back(0, 0)
        far = jnp.where(z >= 6, 1, 0)
        await_a(1)

        @pl.when(far == 1)
        def _():
            await_b(1)
            await_b(3)

        add_up(1, far, multiply(1, 0, far), multiply(1, 1, far))

        @pl.when(far == 0)
        def _():
            await_b(1)
            await_b(3)

        add_up(1, 1 - far, multiply(1, 0, 1 - far), multiply(1, 1, 1 - far))
        send_back(1, far)
        add_up(0, 1, multiply(0, 0, 1), multiply(0, 1, 1))
        send_back(1, 1 - far)
        send_back(0, 1)
        keep = pltpu.make_async_copy(zret.at[z], m_ref.at[z], m_sem)
        keep.start()

        keep.wait()
        sent(c_out, cs_sem)
        sent(a_buf.at[:, pl.ds(0, 3)], as_sem.at[0])
        sent(a_buf.at[:, pl.ds(0, 3)], bs_sem)

        @pl.when(x_core != core)
        def _():
            sent(a_buf.at[0, :, 0], as_sem.at[1])

        sent(zret.at[pl.ds(0, 15)], rs_sem)

    pl.when(in_plane)(product_of_plane)

    @pl.when(in_plane)
    def _():
        sent(zsend.at[pl.ds(0, 7)], zs_sem)

    @pl.when(jnp.logical_not(in_plane))
    def _():
        sent(zsend, zs_sem)

    @pl.when(in_plane)
    def _():
        arrived(zsend.at[pl.ds(0, 7)], rr_sem)

    @pl.when(jnp.logical_not(in_plane))
    def _():
        arrived(zsend, rr_sem)


def time_kernel(m_ref, basis, out, by_cf, timed, o_sem):
    for freq in range(FREQ):
        for part in range(2):
            by_cf[pl.ds((part * FREQ + freq) * 16, 16)] = m_ref[freq, part].astype(F32)
    high, low = split_in_two(basis[...] * (1.0 / math.sqrt(FREQ)))
    weights = jnp.concatenate([high, low])
    pieces = o_sem.shape[0]
    width = 16 // pieces

    def store(piece):
        rows = pl.ds(piece * width, width)
        return pltpu.make_async_copy(timed.at[:, rows], out.at[:, rows], o_sem.at[piece])

    for piece in range(pieces):
        for s in range(piece * width, (piece + 1) * width):
            rows = by_cf[pl.ds(s, 16, stride=16), :].astype(BF16)
            rows = jnp.concatenate([rows, rows])
            values = lax.dot_general(rows, weights, (((0,), (0,)), ((), ())), preferred_element_type=F32)
            timed[:, s] = values.astype(BF16).reshape(4, 32, timed.shape[-1])
        store(piece).start()
    for piece in range(pieces):
        store(piece).wait()


def on_device(traces, taper_weights):
    shots, receivers, samples = traces.shape
    table = fourier_table(samples)
    vmem, anywhere = pl.BlockSpec(memory_space=pltpu.VMEM), pl.BlockSpec(memory_space=pl.ANY)
    dma = pltpu.SemaphoreType.DMA
    product = pl.pallas_call(
        product_kernel,
        out_shape=jax.ShapeDtypeStruct((FREQ, 2, 16, 128), BF16),
        in_specs=[anywhere, vmem],
        out_specs=anywhere,
        scratch_shapes=[
            pltpu.VMEM((4, 16, receivers, samples), BF16),
            pltpu.VMEM((256, 128), F32),
            pltpu.VMEM((FREQ, 2, 16, 128), BF16),
            pltpu.VMEM((16, 2, 16, 128), BF16),
            pltpu.VMEM((4, 2, 2, 32, 128), BF16),
            pltpu.VMEM((2, 4, 2, 2, 2, 32, 128), BF16),
            pltpu.VMEM((4, 2, 2, 4, 32, 128), BF16),
            pltpu.VMEM((2, 2, 2, 64, 128), F32),
            pltpu.VMEM((2, 2, 2, 64, 128), F32),
            pltpu.VMEM((2, 2, 2, 64, 128), F32),
            pltpu.VMEM((16, 2, 16, 128), BF16),
            dma((4,)), dma, dma, dma((4,)), dma((2,)), dma((2,)), dma, dma((4,)),
            dma, dma((2, 2)), dma, dma,
        ],
        compiler_params=pltpu.CompilerParams(
            collective_id=0, has_side_effects=True, vmem_limit_bytes=52 << 20
        ),
        name="product",
    )(traces.reshape(4, 16, receivers, samples), taper_weights.reshape(1, samples))
    timed = pl.pallas_call(
        time_kernel,
        out_shape=jax.ShapeDtypeStruct((4, 16, receivers, samples), BF16),
        in_specs=[vmem, vmem],
        out_specs=anywhere,
        scratch_shapes=[
            pltpu.VMEM((256, 128), F32),
            pltpu.VMEM((4, 16, receivers, samples), BF16),
            dma((4,)),
        ],
        compiler_params=pltpu.CompilerParams(vmem_limit_bytes=52 << 20),
        name="back_to_time",
    )(product, table)
    return timed.reshape(shots, receivers, samples)


def solution(mesh):
    placed = (P("shot", "rcv", None), P())
    return jax.shard_map(
        on_device, mesh=mesh, in_specs=placed, out_specs=P("shot", "rcv", None), check_vma=False
    )
```

```python
import functools
import math

import jax
import jax.numpy as jnp
import numpy as np
from jax import lax
from jax.experimental import pallas as pl
from jax.experimental.pallas import tpu as pltpu
from jax.sharding import PartitionSpec as P

FREQ = 8
MESH = pl.DeviceIdType.MESH
BF16, F32 = jnp.bfloat16, jnp.float32


def fourier_table(samples_count):
    samples = np.arange(samples_count)
    freq_bins = 1 + 3 * np.arange(FREQ)
    phases = 2.0 * math.pi * (freq_bins[:, None] * samples[None, :] % samples_count) / samples_count
    return np.concatenate([np.cos(phases), -np.sin(phases)]).astype(np.float32)


def fourier_rows(samples_count):
    row = lax.broadcasted_iota(jnp.int32, (2 * FREQ, samples_count), 0)
    sample = lax.broadcasted_iota(jnp.int32, (2 * FREQ, samples_count), 1)
    quarters = 1 + row // FREQ
    turns = (1 + 3 * (row % FREQ)) * sample + quarters * (samples_count // 4) + samples_count // 2
    turns = turns % samples_count - samples_count // 2
    return jnp.sin(turns.astype(F32) * (2.0 * math.pi / samples_count))


def place():
    shot, rcv = lax.axis_index("shot"), lax.axis_index("rcv")
    return lax.rem(rcv, 4), lax.rem(shot // 2, 4), shot // 8 * 8 + rcv // 4, lax.rem(shot, 2)


def device(x, y, z, core):
    return (z // 8 * 8 + y * 2 + core, lax.rem(z, 8) * 4 + x)


def ring(value, size):
    return lax.rem(value + size, size)


def split_in_two(value):
    high = value.astype(BF16)
    return high, (value - high.astype(F32)).astype(BF16)


def swap_quarters(tiles):
    quarter = lax.broadcasted_iota(jnp.int32, tiles[0].shape, 1) // 32
    out = []
    for j in range(4):
        total = None
        for i in range(4):
            shift = 32 * ((i - j) % 4)
            moved = pltpu.roll(tiles[i], shift, 1) if shift else tiles[i]
            total = moved if total is None else jnp.where(quarter == i, moved, total)
        out.append(total)
    return out


def product_kernel(
    traces, taper, m_ref,
    tr, by_s, zsend, zin, own, a_buf, b_buf, c_out, c_in, c_own, zret,
    t_sem, m_sem, zs_sem, zr_sem, as_sem, ar_sem, bs_sem, br_sem, cs_sem, cr_sem, rs_sem, rr_sem,
):
    x, y, z, core = place()
    in_plane = z < FREQ
    x_half, x_core = lax.rem(x, 2), x // 2
    samples = traces.shape[-1]

    def remote(src, dst, send, recv, target):
        return pltpu.make_async_remote_copy(
            src_ref=src, dst_ref=dst, send_sem=send, recv_sem=recv, device_id=target, device_id_type=MESH
        )

    def arrived(ref, sem):
        remote(ref, ref, sem, sem, device(x, y, z, core)).wait_recv()

    def sent(ref, sem):
        remote(ref, ref, sem, sem, device(x, y, z, core)).wait_send()

    chunks = t_sem.shape[0]
    per_chunk = 16 // chunks

    def load(chunk):
        rows = pl.ds(chunk * per_chunk, per_chunk)
        return pltpu.make_async_copy(traces.at[:, rows], tr.at[:, rows], t_sem.at[chunk])

    for chunk in range(chunks):
        load(chunk).start()

    barrier = pltpu.get_barrier_semaphore()

    def greet(target):
        pl.semaphore_signal(barrier, inc=1, device_id=target, device_id_type=MESH)

    @pl.when(in_plane)
    def _():
        for step in (8, 7, 9, 6, 10, 5, 11, 4, 12, 3, 13, 2, 14, 1, 15):
            greet(device(x, y, lax.rem(z + step, 16), core))
        for step in (2, 1, 3):
            for other in (0, 1):
                greet(device(lax.rem(x + step, 4), y, z, other))
            greet(device(x, lax.rem(y + step, 4), z, core))
        greet(device(x, y, z, 1 - core))

    high, low = split_in_two(fourier_rows(samples) * taper[...] / math.sqrt(samples))
    weights = jnp.concatenate([high, low])
    for s in range(0, 16, 2):
        if s % per_chunk == 0:
            load(s // per_chunk).wait()
        block = jnp.concatenate([tr[:, s], tr[:, s + 1]]).reshape(256, samples)
        both = lax.dot_general(weights, block, (((1,), (1,)), ((), ())), preferred_element_type=F32)
        summed = both[:16] + both[16:]
        by_s[pl.ds(s * 16, 16)] = summed[:, :128]
        by_s[pl.ds(s * 16 + 16, 16)] = summed[:, 128:]
    for freq in range(FREQ):
        for part in range(2):
            zsend[freq, part] = by_s[pl.ds(part * FREQ + freq, 16, stride=16), :].astype(BF16)

    @pl.when(in_plane)
    def _():
        pl.semaphore_wait(barrier, 7 + 9 + 1)

    @pl.when(jnp.logical_not(in_plane))
    def _():
        pl.semaphore_wait(barrier, 8)

    def to_plane(freq):
        return remote(zsend.at[freq], zin.at[z], zs_sem, zr_sem.at[z // 4], device(x, y, freq, core))

    for freq in range(FREQ):

        @pl.when(freq != z)
        def _():
            to_plane(freq).start()

    def product_of_plane():
        zin[z] = zsend[z]

        def a_copy(group, step):
            return remote(
                own.at[group], a_buf.at[x_half, group, core], as_sem.at[0 if step else 1], ar_sem.at[group // 2],
                device(lax.rem(x + step, 4), y, z, x_core),
            )

        def b_copy(group, step):
            return remote(
                own.at[group], b_buf.at[group, :, :, y], bs_sem, br_sem.at[group],
                device(x, lax.rem(y + step, 4), z, core),
            )

        def arrange(group):
            @pl.when(group == z // 4)
            def _():
                arrived(zin.at[pl.ds(0, 3)], zr_sem.at[group])

            @pl.when(group != z // 4)
            def _():
                arrived(zin.at[pl.ds(0, 4)], zr_sem.at[group])

            for part in range(2):
                tiles = swap_quarters([zin[group * 4 + i, part].astype(F32) for i in range(4)])
                for j in range(4):
                    tile = tiles[j].astype(BF16)
                    rows = pl.ds(j % 2 * 16, 16)
                    own[group, part, j // 2, rows] = tile
                    b_buf[group, part, j // 2, y, rows] = tile
        def send_a(group):
            for step in (2, 1, 3):
                a_copy(group, step).start()

            @pl.when(x_core != core)
            def _():
                a_copy(group, 0).start()

            @pl.when(x_core == core)
            def _():
                a_buf[x_half, group, core] = own[group]

        def send_b(group):
            for step in (2, 1, 3):
                b_copy(group, step).start()

        def await_a(late):
            @pl.when(x_core == core)
            def _():
                arrived(a_buf.at[:, pl.ds(0, 3), 0], ar_sem.at[late])

            @pl.when(x_core != core)
            def _():
                arrived(a_buf.at[:, pl.ds(0, 2)], ar_sem.at[late])

        def await_b(group):
            arrived(a_buf.at[0, pl.ds(0, 3), 0], br_sem.at[group])

        def right(deep, wide):
            return jnp.concatenate(
                [
                    jnp.concatenate([b_buf[2 * deep + wide, part, half].reshape(128, 128) for part in range(2)], axis=1)
                    for half in range(2)
                ]
            )

        def left(upper, deep):
            return jnp.concatenate(
                [
                    jnp.concatenate(
                        [a_buf[half, 2 * upper + deep, rows_of, part].reshape(64, 128) for half in range(2)], axis=1
                    )
                    for rows_of in (1 - core, core)
                    for part in range(2)
                ]
            )

        def multiply(upper, deep, wide):
            both = jnp.dot(left(upper, deep), right(deep, wide), preferred_element_type=F32)
            by_real, by_imag = both[:, :128], both[:, 128:]
            out = []
            for at in (0, 128):
                out.append(by_real[at : at + 64] - by_imag[at + 64 : at + 128])
                out.append(by_imag[at : at + 64] + by_real[at + 64 : at + 128])
            return out

        def to_partner(upper, wide):
            return remote(
                c_out.at[upper, wide], c_in.at[upper, wide], cs_sem, cr_sem.at[upper, wide], device(x, y, z, 1 - core)
            )

        def back(target):
            return remote(zret.at[target], m_ref.at[z], rs_sem, rr_sem, device(x, y, target, core))

        def send_back(upper, wide):
            arrived(c_in.at[upper, wide], cr_sem.at[upper, wide])
            group = 2 * upper + wide
            for part in range(2):
                tiles = []
                for j in range(4):
                    at = (upper, wide, part, pl.ds(j * 16, 16))
                    tiles.append(c_own[at] + c_in[at])
                tiles = swap_quarters(tiles)
                for i in range(4):
                    zret[group * 4 + i, part] = (tiles[i] * (1.0 / 32.0)).astype(BF16)
            for i in range(4):
                target = group * 4 + i

                @pl.when(target != z)
                def _():
                    back(target).start()

        def add_up(upper, wide, first, second):
            for part in range(2):
                c_out[upper, wide, part] = first[part] + second[part]
            to_partner(upper, wide).start()
            for part in range(2):
                c_own[upper, wide, part] = first[2 + part] + second[2 + part]

        @pl.loop(0, 2)
        def _(index):
            group = (z // 4) ^ index
            arrange(group)

            @pl.when(group == 0)
            def _():
                send_b(group)

            send_a(group)

        arrange(2)
        send_b(2)
        send_a(2)
        send_b(1)
        arrange(3)
        send_a(3)
        send_b(3)

        await_a(0)
        await_b(0)
        first = multiply(0, 0, 0)
        await_b(2)
        add_up(0, 0, first, multiply(0, 1, 0))
        send_back(0, 0)
        far = jnp.where(z >= 6, 1, 0)
        await_a(1)

        @pl.when(far == 1)
        def _():
            await_b(1)
            await_b(3)

        add_up(1, far, multiply(1, 0, far), multiply(1, 1, far))

        @pl.when(far == 0)
        def _():
            await_b(1)
            await_b(3)

        add_up(1, 1 - far, multiply(1, 0, 1 - far), multiply(1, 1, 1 - far))
        send_back(1, far)
        add_up(0, 1, multiply(0, 0, 1), multiply(0, 1, 1))
        send_back(1, 1 - far)
        send_back(0, 1)
        keep = pltpu.make_async_copy(zret.at[z], m_ref.at[z], m_sem)
        keep.start()

        keep.wait()
        sent(c_out, cs_sem)
        sent(a_buf.at[:, pl.ds(0, 3)], as_sem.at[0])
        sent(a_buf.at[:, pl.ds(0, 3)], bs_sem)

        @pl.when(x_core != core)
        def _():
            sent(a_buf.at[0, :, 0], as_sem.at[1])

        sent(zret.at[pl.ds(0, 15)], rs_sem)

    pl.when(in_plane)(product_of_plane)

    @pl.when(in_plane)
    def _():
        sent(zsend.at[pl.ds(0, 7)], zs_sem)

    @pl.when(jnp.logical_not(in_plane))
    def _():
        sent(zsend, zs_sem)

    @pl.when(in_plane)
    def _():
        arrived(zsend.at[pl.ds(0, 7)], rr_sem)

    @pl.when(jnp.logical_not(in_plane))
    def _():
        arrived(zsend, rr_sem)


def time_kernel(m_ref, basis, out, by_cf, timed, o_sem):
    for freq in range(FREQ):
        for part in range(2):
            by_cf[pl.ds((part * FREQ + freq) * 16, 16)] = m_ref[freq, part].astype(F32)
    high, low = split_in_two(basis[...] * (1.0 / math.sqrt(FREQ)))
    weights = jnp.concatenate([high, low])
    pieces = o_sem.shape[0]
    width = 16 // pieces

    def store(piece):
        rows = pl.ds(piece * width, width)
        return pltpu.make_async_copy(timed.at[:, rows], out.at[:, rows], o_sem.at[piece])

    for piece in range(pieces):
        for s in range(piece * width, (piece + 1) * width):
            rows = by_cf[pl.ds(s, 16, stride=16), :].astype(BF16)
            rows = jnp.concatenate([rows, rows])
            values = lax.dot_general(rows, weights, (((0,), (0,)), ((), ())), preferred_element_type=F32)
            timed[:, s] = values.astype(BF16).reshape(4, 32, timed.shape[-1])
        store(piece).start()
    for piece in range(pieces):
        store(piece).wait()


def on_device(traces, taper_weights):
    shots, receivers, samples = traces.shape
    table = fourier_table(samples)
    vmem, anywhere = pl.BlockSpec(memory_space=pltpu.VMEM), pl.BlockSpec(memory_space=pl.ANY)
    dma = pltpu.SemaphoreType.DMA
    product = pl.pallas_call(
        product_kernel,
        out_shape=jax.ShapeDtypeStruct((FREQ, 2, 16, 128), BF16),
        in_specs=[anywhere, vmem],
        out_specs=anywhere,
        scratch_shapes=[
            pltpu.VMEM((4, 16, receivers, samples), BF16),
            pltpu.VMEM((256, 128), F32),
            pltpu.VMEM((FREQ, 2, 16, 128), BF16),
            pltpu.VMEM((16, 2, 16, 128), BF16),
            pltpu.VMEM((4, 2, 2, 32, 128), BF16),
            pltpu.VMEM((2, 4, 2, 2, 2, 32, 128), BF16),
            pltpu.VMEM((4, 2, 2, 4, 32, 128), BF16),
            pltpu.VMEM((2, 2, 2, 64, 128), F32),
            pltpu.VMEM((2, 2, 2, 64, 128), F32),
            pltpu.VMEM((2, 2, 2, 64, 128), F32),
            pltpu.VMEM((16, 2, 16, 128), BF16),
            dma((2,)), dma, dma, dma((4,)), dma((2,)), dma((2,)), dma, dma((4,)),
            dma, dma((2, 2)), dma, dma,
        ],
        compiler_params=pltpu.CompilerParams(
            collective_id=0, has_side_effects=True, vmem_limit_bytes=52 << 20
        ),
        name="product",
    )(traces.reshape(4, 16, receivers, samples), taper_weights.reshape(1, samples))
    timed = pl.pallas_call(
        time_kernel,
        out_shape=jax.ShapeDtypeStruct((4, 16, receivers, samples), BF16),
        in_specs=[vmem, vmem],
        out_specs=anywhere,
        scratch_shapes=[
            pltpu.VMEM((256, 128), F32),
            pltpu.VMEM((4, 16, receivers, samples), BF16),
            dma((4,)),
        ],
        compiler_params=pltpu.CompilerParams(vmem_limit_bytes=52 << 20),
        name="back_to_time",
    )(product, table)
    return timed.reshape(shots, receivers, samples)


def solution(mesh):
    placed = (P("shot", "rcv", None), P())
    return jax.shard_map(
        on_device, mesh=mesh, in_specs=placed, out_specs=P("shot", "rcv", None), check_vma=False
    )
```
